256 devices in a mesh: ctx: 32 (over z, x_hi, core), tp: 8 (over x_lo, y).
Axes of the slice: x: 4 (x_hi: 2, x_lo: 2; x = x_hi * 2 + x_lo), y: 4, z: 8, core: 2. Of those that a mesh axis runs over, the one named last changes fastest.
Arguments:
- tokens: bfloat16 [32768, 4096], P('ctx', 'tp'), may hold values from -6 to 6
- proj_weight: bfloat16 [4096, 3, 2048], P('ctx', None, 'tp'), may hold values from -0.09375 to 0.09375
- short_taps: float32 [3, 3, 2048], P(None, None, 'tp'), may hold values from -3 to 3
- long_filter: float32 [2048, 32768], P(('tp', 'ctx')), as said below
- skip_gain: float32 [2048], P(('tp', 'ctx')), may hold values from 0.5 to 1.5
Outputs:
- block_output: bfloat16 [32768, 2048], P('ctx', 'tp')
The draws below stay inside these ranges and needn't reach their ends.
Inputs may be any that keep to these rules, and one draw needn't show every extreme that they name: `long_filter`: each channel's taps are scaled so that their squares sum to at most about one.
All inputs are finite; a program needn't handle non-finite values.
Results may differ from the reference program's by a relative error of at most 0.012.
Values may be sent and summed in bfloat16 or wider, within the bound.
No kernel may reach another device: no remote copies, remote signals or barrier semaphores. Data moves between devices by JAX's collectives and lax.ppermute only.
A program may use at most 64 MiB of HBM per device.

```python
import math
import jax
import jax.numpy as jnp
from jax import lax

D = 4096
C = 2048
SHORT = 3
SEQUENCE_TOKENS = 32768


def draw_long_filter(key, part):
    key = jax.random.fold_in(key, 7)
    rate_key, noise_key, location_random_key, retain_random_key = jax.random.split(key, 4)
    slowest = 0.01 / SEQUENCE_TOKENS
    fastest = 1.0 / 40.0
    jitter_values = jax.random.normal(noise_key, (C, SEQUENCE_TOKENS), jnp.float32)
    log_rate = jax.random.uniform(rate_key, (C, 1), jnp.float32, math.log(slowest), math.log(fastest))
    falloff_rates = jnp.exp(log_rate)
    token_positions = jnp.arange(SEQUENCE_TOKENS, dtype=jnp.float32)[None, :]
    spike_amplitude = jnp.sqrt(jnp.expm1(-2.0 * falloff_rates) / jnp.expm1(-2.0 * falloff_rates * SEQUENCE_TOKENS))
    spike_location = jax.random.randint(location_random_key, (4,), 1, SEQUENCE_TOKENS)
    spike_retained = jax.random.uniform(retain_random_key, (4,), jnp.float32, 0.5, 0.8)
    spike_multiplier = jnp.ones((1, SEQUENCE_TOKENS), jnp.float32)
    for spike_index in range(4):
        spike_multiplier = spike_multiplier * jnp.where(jnp.arange(SEQUENCE_TOKENS)[None, :] >= spike_location[spike_index], spike_retained[spike_index], 1.0)
    return (spike_amplitude * jitter_values * jnp.exp(-falloff_rates * token_positions) * spike_multiplier).astype(jnp.float32)


def steps_of(key, shape, pieces, low, high):
    level, own = 1.0, jax.random.fold_in(key, 6)
    for position, blocks in pieces:
        draws = jnp.exp(jax.random.uniform(jax.random.fold_in(own, position), (blocks,), jnp.float32, low / len(pieces), high / len(pieces)))
        level = level * jnp.repeat(draws, shape[position] // blocks).reshape([-1 if axis == position else 1 for axis in range(len(shape))])
    return level


def scatter_about(key, extent, deviation, reach, pieces=(), kind=jnp.bfloat16):
    array = deviation * jax.random.normal(key, extent, jnp.float32)
    if pieces:
        array = array * steps_of(key, extent, pieces, -0.22, 0.18)
    return jnp.clip(array, -reach, reach).astype(kind)


def setup_inputs(seed: int = 0) -> dict:
    keys = jax.random.split(jax.random.key(seed), 6)
    return {
        "tokens": scatter_about(keys[0], (SEQUENCE_TOKENS, D), 1.0, 6.0, ((0, 32), (1, 8))),
        "proj_weight": scatter_about(keys[1], (D, 3, C), D ** -0.5, 0.09375, ((0, 32), (2, 8))),
        "short_taps": scatter_about(keys[2], (SHORT, 3, C), 0.6, 3.0, ((2, 8),), jnp.float32),
        "long_filter": draw_long_filter(jax.random.fold_in(keys[5], 71), 0),
        "skip_gain": jnp.clip(0.5 + 1.0 * jax.random.uniform(keys[4], (C,), jnp.float32) ** steps_of(keys[4], (C,), ((0, 256),), -0.2, 0.2), 0.5, 1.5),
    }


def long_block(inputs_block):
    signal, filters, gains = inputs_block
    seq_len = signal.shape[1]
    padded_len = 2 * seq_len
    spectrum = jnp.fft.rfft(signal, n=padded_len, axis=1) * jnp.fft.rfft(filters, n=padded_len, axis=1)
    result = jnp.fft.irfft(spectrum, n=padded_len, axis=1)[:, :seq_len]
    return result + gains[:, None] * signal


def reference(tokens, proj_weight, short_taps, long_filter, skip_gain):
    seq_len = tokens.shape[0]
    channels = proj_weight.shape[2]
    flat_weights = proj_weight.reshape(proj_weight.shape[0], 3 * channels)
    projected = jnp.dot(tokens, flat_weights, preferred_element_type=jnp.float32).astype(jnp.bfloat16)
    widened = projected.reshape(seq_len, 3, channels).astype(jnp.float32)
    lag_count = short_taps.shape[0]
    padded = jnp.concatenate([jnp.zeros((lag_count - 1, 3, channels), jnp.float32), widened], 0)
    mixed = jnp.zeros((seq_len, 3, channels), jnp.float32)
    for lag_index in range(lag_count):
        first_row = lag_count - 1 - lag_index
        mixed = mixed + short_taps[lag_index] * padded[first_row:first_row + seq_len]
    gate_query = mixed[:, 0].astype(jnp.bfloat16)
    gated_input = (mixed[:, 1] * mixed[:, 2]).astype(jnp.bfloat16)
    block_width = math.gcd(channels, 256)
    block_count = channels // block_width
    signal = gated_input.astype(jnp.float32).T.reshape(block_count, block_width, seq_len)
    filters = long_filter.reshape(block_count, block_width, seq_len)
    gains = skip_gain.reshape(block_count, block_width)
    convolved = lax.map(long_block, (signal, filters, gains))
    convolved = convolved.reshape(channels, seq_len).astype(jnp.bfloat16)
    product = gate_query.astype(jnp.float32) * convolved.T.astype(jnp.float32)
    return product.astype(jnp.bfloat16)
```

```python
import math

import jax
import jax.numpy as jnp
import numpy as np
from jax import lax
from jax.experimental import pallas as pl
from jax.experimental.pallas import tpu as pltpu
from jax.sharding import PartitionSpec as P

F32 = jnp.float32
BF16 = jnp.bfloat16
MIB = 1 << 20
VMEM = 56 * MIB

Z_GROUPS = [[z * 4 + r for z in range(8)] for r in range(4)]
OTHER_CORE = [(i, i ^ 1) for i in range(32)]
OTHER_XLO = [(i, i ^ 4) for i in range(8)]
FROM_UP = [(i, (i & 4) | ((i - 1) & 3)) for i in range(8)]
FROM_DOWN = [(i, (i & 4) | ((i + 1) & 3)) for i in range(8)]
ACROSS = [(i, (i & 4) | ((i + 2) & 3)) for i in range(8)]
ROWS = 1024
HALF = 512
OWN = 384
FOUR_GROUPS = [[z * 4 + r for r in range(4)] for z in range(8)]
HALO = 16
OUTER = 128
INNER = 256


def other_xlo(x):
    return lax.ppermute(x, "tp", OTHER_XLO)


def from_up(x):
    return lax.ppermute(x, "tp", FROM_UP)


def from_down(x):
    return lax.ppermute(x, "tp", FROM_DOWN)


def tied(*xs):
    return lax.optimization_barrier(xs)


def dot(a, b):
    return jnp.dot(a, b, preferred_element_type=F32)


def vmem_specs(count):
    return [pl.BlockSpec(memory_space=pltpu.VMEM)] * count


def whole(shape):
    return pl.BlockSpec(shape, lambda r: (0,) * len(shape))


def tile(rows, cols):
    return pl.BlockSpec((rows, cols), lambda r: (r, 0))


def halves(cols):
    return [
        pl.BlockSpec((256, cols), lambda r: (jnp.minimum(r, 1), 0)),
        pl.BlockSpec((256, cols), lambda r: (jnp.maximum(r - 2, 0), 0)),
    ]


def for_each_half(step):
    r = pl.program_id(0)
    pl.when(r < 2)(lambda: step(0))
    pl.when(r >= 2)(lambda: step(1))


def partial_kernel(places, *refs):
    units, (last_ref, w_ref, out_ref, rim_ref) = refs[:14], refs[14:]

    def step(half):
        total = dot(units[half][...], w_ref[places[0]])
        for u in range(1, 7):
            total += dot(units[2 * u + half][...], w_ref[places[u]])
        out_ref[...] = total

    for_each_half(step)

    @pl.when(pl.program_id(0) == 3)
    def _():
        rim = out_ref[256 - HALO :, :256] + dot(last_ref[...], w_ref[places[7], :, :256])
        rim_ref[...] = rim.astype(BF16)


def partial_products(places, units, last_rows, w):
    return pl.pallas_call(
        partial_kernel,
        grid=(4,),
        out_shape=(
            jax.ShapeDtypeStruct((ROWS, OWN), F32),
            jax.ShapeDtypeStruct((HALO, 256), BF16),
        ),
        in_specs=[pl.BlockSpec(memory_space=pltpu.SMEM)]
        + halves(512) * 7
        + [whole((HALO, 512)), whole((8, 512, OWN))],
        out_specs=(tile(256, OWN), whole((HALO, 256))),
        compiler_params=pltpu.CompilerParams(vmem_limit_bytes=VMEM),
        cost_estimate=pl.CostEstimate(
            flops=2 * 7 * 1024 * 512 * OWN, bytes_accessed=11 * MIB, transcendentals=0
        ),
    )(places, *units, last_rows, w)


def rim_kernel(places, *refs):
    units, (w_ref, out_ref) = refs[:8], refs[8:]
    total = dot(units[0][...], w_ref[places[0], :, :256])
    for u in range(1, 8):
        total += dot(units[u][...], w_ref[places[u], :, :256])
    out_ref[...] = total.astype(BF16)


def rim_rows(places, units, last_rows, w):
    last = HALF // HALO - 1
    return pl.pallas_call(
        rim_kernel,
        grid=(1,),
        out_shape=jax.ShapeDtypeStruct((HALO, 256), BF16),
        in_specs=[pl.BlockSpec(memory_space=pltpu.SMEM)]
        + [pl.BlockSpec((HALO, 512), lambda r: (last, 0))] * 7
        + [whole((HALO, 512)), whole((8, 512, OWN))],
        out_specs=whole((HALO, 256)),
        compiler_params=pltpu.CompilerParams(vmem_limit_bytes=VMEM),
        cost_estimate=pl.CostEstimate(
            flops=2 * 8 * 256 * 512 * 256, bytes_accessed=4 * MIB, transcendentals=0
        ),
    )(places, *units[1::2], last_rows, w)


def filtered(scratch, branch, taps, start, size):
    total = taps[0:1, :] * scratch[branch, pl.ds(HALO + start, size), :]
    for lag in (1, 2):
        total = total + taps[lag : lag + 1, :] * scratch[branch, pl.ds(HALO + start - lag, size), :]
    return total


def gated_kernel(places, *refs):
    units, (acc_ref, own_ref, sib_ref, rim_ref, taps_ref, out_ref, scratch) = refs[:16], refs[16:]
    r = pl.program_id(0)

    @pl.when(r == 0)
    def _():
        scratch[0, 0:HALO, :] = rim_ref[:, :256].astype(F32)
        scratch[1, 0:HALO, :] = rim_ref[:, 256:].astype(F32)

    @pl.when(r > 0)
    def _():
        scratch[:, 0:HALO, :] = scratch[:, 256 : 256 + HALO, :]

    def step(half):
        own = acc_ref[:, :256] + dot(units[14 + half][...], own_ref[0, :, :256])
        scratch[0, HALO:, :] = own.astype(BF16).astype(F32)
        sib = dot(units[half][...], sib_ref[places[0], :, :256])
        for u in range(1, 8):
            sib += dot(units[2 * u + half][...], sib_ref[places[u], :, :256])
        scratch[1, HALO:, :] = sib.astype(BF16).astype(F32)

    for_each_half(step)
    a = filtered(scratch, 0, taps_ref[0], 0, 256)
    b = filtered(scratch, 1, taps_ref[1], 0, 256)
    out_ref[...] = (a * b).T.reshape(32, 8, 256).astype(BF16)


def gated_input(places, units, acc, own, sib, rim, taps):
    specs = (
        [pl.BlockSpec((256, 512), lambda r, p: (jnp.minimum(r, 1), 0)),
         pl.BlockSpec((256, 512), lambda r, p: (jnp.maximum(r - 2, 0), 0))] * 8
        + [
            pl.BlockSpec((256, OWN), lambda r, p: (r, 0)),
            pl.BlockSpec((1, 512, OWN), lambda r, p: (p[7], 0, 0)),
            pl.BlockSpec((8, 512, OWN), lambda r, p: (0, 0, 0)),
            pl.BlockSpec((HALO, 512), lambda r, p: (0, 0)),
            pl.BlockSpec((2, 3, 256), lambda r, p: (0, 0, 0)),
        ]
    )
    return pl.pallas_call(
        gated_kernel,
        out_shape=jax.ShapeDtypeStruct((32, 8, ROWS), BF16),
        grid_spec=pltpu.PrefetchScalarGridSpec(
            num_scalar_prefetch=1,
            grid=(4,),
            in_specs=specs,
            out_specs=pl.BlockSpec((32, 8, 256), lambda r, p: (0, 0, r)),
            scratch_shapes=[pltpu.VMEM((2, HALO + 256, 256), F32)],
        ),
        compiler_params=pltpu.CompilerParams(vmem_limit_bytes=VMEM),
        cost_estimate=pl.CostEstimate(
            flops=2 * 9 * 1024 * 512 * 256, bytes_accessed=13 * MIB, transcendentals=0
        ),
    )(places, *units, acc, own, sib, rim, taps)


def query_kernel(places, even, *refs):
    units, (acc_ref, own_ref, sib_ref, out_ref) = refs[:16], refs[16:]

    def step(half):
        own = acc_ref[:, 256:] + dot(units[14 + half][...], own_ref[0, :, 256:])
        sib = dot(units[half][...], sib_ref[places[0]])
        for u in range(1, 8):
            sib += dot(units[2 * u + half][...], sib_ref[places[u]])
        first_core = even[0] == 1
        left = jnp.where(first_core, own, sib)
        right = jnp.where(first_core, sib, own)
        out_ref[...] = jnp.concatenate([left, right], 1).astype(BF16)

    for_each_half(step)


def query_rows(places, even, units, acc, own, sib):
    specs = (
        [pl.BlockSpec((256, 512), lambda r, p, e: (jnp.minimum(r, 1), 0)),
         pl.BlockSpec((256, 512), lambda r, p, e: (jnp.maximum(r - 2, 0), 0))] * 8
        + [
            pl.BlockSpec((256, OWN), lambda r, p, e: (r, 0)),
            pl.BlockSpec((1, 512, OWN), lambda r, p, e: (p[7], 0, 0)),
            pl.BlockSpec((8, 512, 128), lambda r, p, e: (0, 0, 2)),
        ]
    )
    return pl.pallas_call(
        query_kernel,
        out_shape=jax.ShapeDtypeStruct((ROWS, 256), BF16),
        grid_spec=pltpu.PrefetchScalarGridSpec(
            num_scalar_prefetch=2,
            grid=(4,),
            in_specs=specs,
            out_specs=pl.BlockSpec((256, 256), lambda r, p, e: (r, 0)),
        ),
        compiler_params=pltpu.CompilerParams(vmem_limit_bytes=VMEM),
        cost_estimate=pl.CostEstimate(
            flops=2 * 9 * 1024 * 512 * 128, bytes_accessed=16 * MIB, transcendentals=0
        ),
    )(places, even, *units, acc, own, sib)


def gate_kernel(query_ref, rim_ref, taps_ref, out_ref, scratch):
    scratch[0, 0:HALO, :] = rim_ref[...].astype(F32)
    scratch[0, HALO:, :] = query_ref[...].astype(F32)
    for r in range(ROWS // 256):
        out_ref[r * 256 : r * 256 + 256, :] = filtered(scratch, 0, taps_ref[...], r * 256, 256).astype(BF16)


def query_gate(query, rim, taps):
    return pl.pallas_call(
        gate_kernel,
        out_shape=jax.ShapeDtypeStruct((ROWS, 256), BF16),
        in_specs=vmem_specs(3),
        out_specs=pl.BlockSpec(memory_space=pltpu.VMEM),
        scratch_shapes=[pltpu.VMEM((1, HALO + ROWS, 256), F32)],
        compiler_params=pltpu.CompilerParams(vmem_limit_bytes=VMEM),
        cost_estimate=pl.CostEstimate(flops=1024 * 256 * 6, bytes_accessed=MIB, transcendentals=0),
    )(query, rim, taps)


def two_parts(table):
    high = table.astype(BF16)
    return np.stack([high, (table - high.astype(np.float64)).astype(BF16)])


def tables():
    a = np.arange(OUTER, dtype=np.float64)
    b = np.arange(INNER, dtype=np.float64)
    outer = 2 * np.pi / OUTER * np.outer(a + 0.25, a)
    first = np.concatenate([np.cos(outer), -np.sin(outer)], 0)
    order = (4 * np.arange(32)[None, :] + np.arange(4)[:, None]).reshape(-1)
    inner = 2 * np.pi / INNER * (np.outer(b, b) % INNER)
    turn = np.concatenate([np.cos(inner), np.sin(inner)], 1)
    twist = 2 * np.pi / (OUTER * INNER) * np.outer(a + 0.25, b)
    twiddle = np.stack([np.cos(twist), np.sin(twist)]).astype(np.float32)
    shuffled = first[:, order].astype(BF16)
    packed = np.concatenate([turn.astype(BF16), shuffled, np.concatenate([shuffled[:, :].T, np.zeros((128, 256), BF16)], 0)], 1)
    return two_parts(first), two_parts(turn), packed, twiddle


def split_value(x):
    high = x.astype(BF16)
    return high, (x - high.astype(F32)).astype(BF16)


def turned_forward(wave, c, s):
    real, imag = wave[:OUTER], wave[OUTER:]
    return jnp.concatenate([real * c + imag * s, imag * c - real * s], 0)


def joined_forward(r):
    return r[:OUTER, :INNER] + r[OUTER:, INNER:], r[OUTER:, :INNER] - r[:OUTER, INNER:]


def filter_kernel(h_ref, first_ref, turn_ref, twiddle_ref, out_ref):
    c, s = twiddle_ref[0], twiddle_ref[1]

    def step(ch, carry):
        high, low = split_value(h_ref[ch])
        wave = dot(first_ref[0], high) + (dot(first_ref[1], high) + dot(first_ref[0], low))
        high, low = split_value(turned_forward(wave, c, s))
        wave = dot(high, turn_ref[0]) + (dot(high, turn_ref[1]) + dot(low, turn_ref[0]))
        out_ref[ch] = jnp.concatenate(joined_forward(wave), 0) * (1.0 / (OUTER * INNER))
        return carry

    lax.fori_loop(0, 8, step, 0)


def filter_spectrum(h, first, turn, twiddle):
    return pl.pallas_call(
        filter_kernel,
        out_shape=jax.ShapeDtypeStruct((8, 2 * OUTER, INNER), F32),
        in_specs=vmem_specs(4),
        out_specs=pl.BlockSpec(memory_space=pltpu.VMEM),
        compiler_params=pltpu.CompilerParams(vmem_limit_bytes=VMEM),
        cost_estimate=pl.CostEstimate(
            flops=2 * 3 * 8 * (128 * 256 * 256 + 256 * 256 * 512), bytes_accessed=5 * MIB, transcendentals=0
        ),
    )(h, first, turn, twiddle)


def convolve_kernel(x_ref, h_ref, gain_ref, table_ref, twiddle_ref, out_ref, wide, result):
    c, s = twiddle_ref[0], twiddle_ref[1]
    turn, first, last = table_ref[:, :512], table_ref[:, 512:640], table_ref[:128, 640:]
    wide[...] = x_ref[...].astype(F32)
    for ch in range(8):
        row = wide[:, ch, :]
        x = jnp.concatenate([row[:, q * 256 : q * 256 + 256] for q in range(4)], 0).astype(BF16)
        turned = turned_forward(dot(first, x), c, s).astype(BF16)
        xr, xi = joined_forward(dot(turned, turn))
        hr, hi = h_ref[ch, :OUTER], h_ref[ch, OUTER:]
        product = jnp.concatenate([xr * hr - xi * hi, xr * hi + xi * hr], 0).astype(BF16)
        r = dot(product, turn)
        br = r[:OUTER, :INNER] - r[OUTER:, INNER:]
        bi = r[:OUTER, INNER:] + r[OUTER:, :INNER]
        back = jnp.concatenate([br * c - bi * s, bi * c + br * s], 0).astype(BF16)
        y = dot(last, back)
        result[:, ch, :] = jnp.concatenate([y[q * 32 : q * 32 + 32] for q in range(4)], 1)
    out_ref[...] = (result[...] + gain_ref[...][None] * wide[...]).astype(BF16)


def convolve(x, h, gain, table, twiddle):
    return pl.pallas_call(
        convolve_kernel,
        out_shape=jax.ShapeDtypeStruct((32, 8, ROWS), BF16),
        in_specs=vmem_specs(5),
        out_specs=pl.BlockSpec(memory_space=pltpu.VMEM),
        scratch_shapes=[pltpu.VMEM((32, 8, ROWS), F32)] * 2,
        compiler_params=pltpu.CompilerParams(vmem_limit_bytes=VMEM),
        cost_estimate=pl.CostEstimate(
            flops=2 * 8 * 2 * (128 * 256 * 256 + 256 * 256 * 512), bytes_accessed=5 * MIB, transcendentals=0
        ),
    )(x, h, gain, table, twiddle)


def finish_kernel(conv_ref, gate_ref, out_ref):
    for r in range(ROWS // 256):
        cols = slice(r * 256, r * 256 + 256)
        conv = conv_ref[:, :, cols].astype(F32).reshape(256, 256).T
        out_ref[cols, :] = (conv * gate_ref[cols, :].astype(F32)).astype(BF16)


def finish(conv, gate):
    return pl.pallas_call(
        finish_kernel,
        out_shape=jax.ShapeDtypeStruct((ROWS, 256), BF16),
        in_specs=vmem_specs(2),
        out_specs=pl.BlockSpec(memory_space=pltpu.VMEM),
        compiler_params=pltpu.CompilerParams(vmem_limit_bytes=VMEM),
        cost_estimate=pl.CostEstimate(flops=1024 * 256, bytes_accessed=2 * MIB, transcendentals=0),
    )(conv, gate)


def next_shard(x):
    return lax.ppermute(x, "ctx", [(i, i + 1) for i in range(31)])


def body(tokens, proj_weight, short_taps, long_filter, skip_gain):
    ctx, tp = lax.axis_index("ctx"), lax.axis_index("tp")
    even = ctx % 2 == 0
    first, turn, packed, twiddle = (jnp.asarray(t) for t in tables())

    near = lax.all_gather(proj_weight.transpose(1, 0, 2), "ctx", axis_index_groups=FOUR_GROUPS)
    q, k, v = (near[:, g].reshape(512, 256) for g in range(3))
    block = jnp.concatenate([jnp.where(even, k, v), jnp.where(even, q[:, :128], q[:, 128:])], 1)
    own = lax.all_gather(block, "ctx", axis_index_groups=Z_GROUPS)

    spectrum = filter_spectrum(long_filter.reshape(8, OUTER, INNER), first, turn, twiddle)
    a0 = (tokens[:HALF], tokens[HALF:])
    ap, am, b0 = zip(*(tied(from_up(t), from_down(t), other_xlo(t)) for t in a0))
    bp, bm, a2 = zip(*(tied(other_xlo(p), from_down(b), from_up(p)) for p, b in zip(ap, b0)))
    rim_b2 = lax.ppermute(b0[1][HALF - HALO :], "tp", ACROSS)
    b2 = (from_up(bp[0]), from_down(bm[1]))
    own, spectrum, a2, bp, bm = tied(own, spectrum, a2, bp, bm)

    xlo, y = tp // 4, tp % 4
    mine, others = xlo * 4, (1 - xlo) * 4
    shift = lambda n: (y + n) % 4
    places = jnp.stack(
        [
            mine + y,
            mine + shift(1),
            mine + shift(3),
            others + y,
            others + shift(1),
            others + shift(3),
            mine + shift(2),
            others + shift(2),
        ]
    ).astype(jnp.int32)
    sib = lax.ppermute(own, "ctx", OTHER_CORE)
    units = (*a0, *ap, *am, *b0, *bp, *bm, *a2)
    acc, rim_own = partial_products(places, units, rim_b2, own)
    rim = next_shard(jnp.concatenate([rim_rows(places, units, rim_b2, sib), rim_own], 1))
    taps = short_taps.transpose(1, 0, 2)
    taps_kv = jnp.where(even, taps[1:3], taps[2:0:-1])
    gated = gated_input(places, units + b2, acc, own, sib, rim, taps_kv)

    owned = lax.all_to_all(gated, "ctx", 0, 0)
    convolved = convolve(owned, spectrum, skip_gain[:, None], packed, twiddle)
    returned = lax.all_to_all(convolved, "ctx", 0, 0)

    flag = even.astype(jnp.int32).reshape(1)
    query = query_rows(places, flag, units + b2, acc, own, sib)
    gate = query_gate(query, next_shard(query[ROWS - HALO :]), taps[0])
    return finish(returned, gate)


def solution(mesh):
    placed = (
        P("ctx", "tp"),
        P("ctx", None, "tp"),
        P(None, None, "tp"),
        P(("tp", "ctx"), None),
        P(("tp", "ctx")),
    )
    return jax.shard_map(
        body, mesh=mesh, in_specs=placed, out_specs=P("ctx", "tp"), check_vma=False
    )
```

```python
import functools

import jax
import jax.numpy as jnp
import numpy as np
from jax import lax
from jax.experimental import pallas as pl
from jax.experimental.pallas import tpu as pltpu
from jax.sharding import PartitionSpec as P

F32 = jnp.float32
BF16 = jnp.bfloat16
MIB = 1 << 20
VMEM = 56 * MIB

FROM_ABOVE = [(i, (i - 4) % 32) for i in range(32)]
FROM_BELOW = [(i, (i + 4) % 32) for i in range(32)]
OTHER_CORE = [(i, i ^ 1) for i in range(32)]
OTHER_XHI = [(i, i ^ 2) for i in range(32)]
OTHER_XLO = [(i, i ^ 4) for i in range(8)]
FROM_UP = [(i, (i & 4) | ((i - 1) & 3)) for i in range(8)]
FROM_DOWN = [(i, (i & 4) | ((i + 1) & 3)) for i in range(8)]
ROWS = 1024
HALF = 512
FOUR_GROUPS = [[z * 4 + r for r in range(4)] for z in range(8)]
HALO = 16
AHEAD = 8
KV = pl.ds(0, 256)
QUERY = pl.ds(256, 128)
OUTER = 128
INNER = 256


def other_xlo(x):
    return lax.ppermute(x, "tp", OTHER_XLO)


def from_up(x):
    return lax.ppermute(x, "tp", FROM_UP)


def from_down(x):
    return lax.ppermute(x, "tp", FROM_DOWN)


def from_above(x):
    return lax.ppermute(x, "ctx", FROM_ABOVE)


def from_below(x):
    return lax.ppermute(x, "ctx", FROM_BELOW)


def tied(*xs):
    return lax.optimization_barrier(xs)


def dot(a, b):
    return jnp.dot(a, b, preferred_element_type=F32)


def vmem_specs(count):
    return [pl.BlockSpec(memory_space=pltpu.VMEM)] * count


def unit_copies(places, u, units, weights, a_buf, b_buf, w_bufs, sems):
    unit = units[u]
    if len(unit) == 1:
        a, b = unit[0].at[pl.ds(0, HALF)], unit[0].at[pl.ds(HALF, HALF + HALO)]
    else:
        a, b = unit
    pairs = [(a, a_buf.at[u]), (b, b_buf.at[u])]
    pairs += [(w.at[places[u], :, cols], buf.at[u]) for (w, cols), buf in zip(weights, w_bufs)]
    return [pltpu.make_async_copy(*pair, sems.at[u, n]) for n, pair in enumerate(pairs)]


def grouped(refs, sizes):
    refs = list(refs)
    return [[refs.pop(0) for _ in range(size)] for size in sizes], refs


def flat(units):
    return [array for unit in units for array in unit]


def add_products(total, first, a, b, w):
    low = dot(a, w)
    high = dot(b, w)
    for rows, value in (
        (slice(HALO, HALO + HALF), low),
        (slice(HALO + HALF, HALO + ROWS), high[:HALF]),
        (slice(0, HALO), high[HALF:]),
    ):
        total[rows, :] = value if first else total[rows, :] + value


def sum_units(places, count, units, weights, joined, total, a_buf, b_buf, w_bufs, sems, others=()):
    copies = [
        unit_copies(places, u, units, weights, a_buf, b_buf, w_bufs, sems) for u in range(count)
    ]
    for u in range(min(AHEAD, count)):
        for copy in copies[u]:
            copy.start()
    for copy in others:
        copy.start()
    for u in range(count):
        if u + AHEAD < count:
            for copy in copies[u + AHEAD]:
                copy.start()
        for copy in copies[u]:
            copy.wait()
        add_products(total, u == 0, a_buf[u], b_buf[u], joined([buf[u] for buf in w_bufs]))


def unit_scratch(count, widths):
    return [
        pltpu.VMEM((count, HALF, 512), BF16),
        pltpu.VMEM((count, HALF + HALO, 512), BF16),
        *[pltpu.VMEM((count, 512, width), BF16) for width in widths],
        pltpu.SemaphoreType.DMA((count, 2 + len(widths))),
    ]


ANY = pl.BlockSpec(memory_space=pl.ANY)
SMEM = pl.BlockSpec(memory_space=pltpu.SMEM)


def partial_kernel(sizes, places, *refs):
    units, (w_ref, out_ref, a_buf, b_buf, w_buf, sems) = grouped(refs, sizes)
    sum_units(places, 7, units, [(w_ref, KV)], lambda w: w[0], out_ref, a_buf, b_buf, [w_buf], sems)


def partial_products(places, units, w):
    return pl.pallas_call(
        functools.partial(partial_kernel, [len(unit) for unit in units]),
        out_shape=jax.ShapeDtypeStruct((HALO + ROWS, 256), F32),
        in_specs=[SMEM] + [ANY] * (len(flat(units)) + 1),
        out_specs=pl.BlockSpec(memory_space=pltpu.VMEM),
        scratch_shapes=unit_scratch(7, [256]),
        compiler_params=pltpu.CompilerParams(vmem_limit_bytes=VMEM),
        cost_estimate=pl.CostEstimate(
            flops=2 * 7 * 1024 * 512 * 256, bytes_accessed=11 * MIB, transcendentals=0
        ),
    )(places, *flat(units), w)


def filtered(branch, taps, start, size):
    total = taps[0:1, :] * branch[pl.ds(HALO + start, size), :]
    for lag in (1, 2):
        total = total + taps[lag : lag + 1, :] * branch[pl.ds(HALO + start - lag, size), :]
    return total


def rounded(branch):
    branch[...] = branch[...].astype(BF16).astype(F32)


def gated_kernel(sizes, places, *refs):
    units, refs = grouped(refs, sizes)
    acc_ref, own_ref, sib_ref, taps_ref, out_ref, a_buf, b_buf, w_buf, sems = refs[:9]
    own_buf, own_sems, mine, theirs = refs[9:]
    copies = [
        pltpu.make_async_copy(acc_ref, mine, own_sems.at[0]),
        pltpu.make_async_copy(own_ref.at[places[7], :, KV], own_buf, own_sems.at[1]),
    ]
    sum_units(places, 8, units, [(sib_ref, KV)], lambda w: w[0], theirs, a_buf, b_buf, [w_buf], sems, copies)
    for copy in copies:
        copy.wait()
    add_products(mine, False, a_buf[7], b_buf[7], own_buf[...])
    rounded(mine)
    rounded(theirs)
    for r in range(ROWS // 256):
        a = filtered(mine, taps_ref[0], r * 256, 256)
        b = filtered(theirs, taps_ref[1], r * 256, 256)
        out_ref[:, :, r * 256 : r * 256 + 256] = (a * b).T.reshape(32, 8, 256).astype(BF16)


def gated_input(places, units, acc, own, sib, taps):
    return pl.pallas_call(
        functools.partial(gated_kernel, [len(unit) for unit in units]),
        out_shape=jax.ShapeDtypeStruct((32, 8, ROWS), BF16),
        in_specs=[SMEM] + [ANY] * (len(flat(units)) + 3) + vmem_specs(1),
        out_specs=pl.BlockSpec(memory_space=pltpu.VMEM),
        scratch_shapes=unit_scratch(8, [256])
        + [
            pltpu.VMEM((512, 256), BF16),
            pltpu.SemaphoreType.DMA((2,)),
            pltpu.VMEM((HALO + ROWS, 256), F32),
            pltpu.VMEM((HALO + ROWS, 256), F32),
        ],
        compiler_params=pltpu.CompilerParams(vmem_limit_bytes=VMEM),
        cost_estimate=pl.CostEstimate(
            flops=2 * 9 * 1024 * 512 * 256, bytes_accessed=13 * MIB, transcendentals=0
        ),
    )(places, *flat(units), acc, own, sib, taps)


def query_kernel(sizes, places, even, *refs):
    units, refs = grouped(refs, sizes)
    own_ref, sib_ref, taps_ref, out_ref, a_buf, b_buf, own_buf, sib_buf, sems, total = refs
    first_core = even[0] == 1

    def joined(w):
        own, sib = w
        return jnp.concatenate([jnp.where(first_core, own, sib), jnp.where(first_core, sib, own)], 1)

    sum_units(places, 8, units, [(own_ref, QUERY), (sib_ref, QUERY)], joined, total, a_buf, b_buf, [own_buf, sib_buf], sems)
    rounded(total)
    for r in range(ROWS // 256):
        out_ref[r * 256 : r * 256 + 256, :] = filtered(total, taps_ref[...], r * 256, 256).astype(BF16)


def query_gate(places, even, units, own, sib, taps):
    return pl.pallas_call(
        functools.partial(query_kernel, [len(unit) for unit in units]),
        out_shape=jax.ShapeDtypeStruct((ROWS, 256), BF16),
        in_specs=[SMEM] * 2 + [ANY] * (len(flat(units)) + 2) + vmem_specs(1),
        out_specs=pl.BlockSpec(memory_space=pltpu.VMEM),
        scratch_shapes=unit_scratch(8, [128, 128]) + [pltpu.VMEM((HALO + ROWS, 256), F32)],
        compiler_params=pltpu.CompilerParams(vmem_limit_bytes=VMEM),
        cost_estimate=pl.CostEstimate(
            flops=2 * 8 * 1024 * 512 * 256, bytes_accessed=12 * MIB, transcendentals=0
        ),
    )(places, even, *flat(units), own, sib, taps)


def two_parts(table):
    high = table.astype(BF16)
    return np.stack([high, (table - high.astype(np.float64)).astype(BF16)])


def tables():
    a = np.arange(OUTER, dtype=np.float64)
    b = np.arange(INNER, dtype=np.float64)
    outer = 2 * np.pi / OUTER * np.outer(a + 0.25, a)
    first = np.concatenate([np.cos(outer), -np.sin(outer)], 0)
    order = (4 * np.arange(32)[None, :] + np.arange(4)[:, None]).reshape(-1)
    inner = 2 * np.pi / INNER * (np.outer(b, b) % INNER)
    turn = np.concatenate([np.cos(inner), np.sin(inner)], 1)
    twist = 2 * np.pi / (OUTER * INNER) * np.outer(a + 0.25, b)
    twiddle = np.stack([np.cos(twist), np.sin(twist)]).astype(np.float32)
    shuffled = first[:, order].astype(BF16)
    packed = np.concatenate([turn.astype(BF16), shuffled, np.concatenate([shuffled[:, :].T, np.zeros((128, 256), BF16)], 0)], 1)
    return two_parts(first), two_parts(turn), packed, twiddle


def split_value(x):
    high = x.astype(BF16)
    return high, (x - high.astype(F32)).astype(BF16)


def turned_forward(wave, c, s):
    real, imag = wave[:OUTER], wave[OUTER:]
    return jnp.concatenate([real * c + imag * s, imag * c - real * s], 0)


def joined_forward(r):
    return r[:OUTER, :INNER] + r[OUTER:, INNER:], r[OUTER:, :INNER] - r[:OUTER, INNER:]


def filter_kernel(h_ref, first_ref, turn_ref, twiddle_ref, out_ref, work):
    c, s = twiddle_ref[0], twiddle_ref[1]
    for ch in range(8):
        high, low = split_value(h_ref[ch])
        wave = dot(first_ref[0], high) + (dot(first_ref[1], high) + dot(first_ref[0], low))
        work[0, ch], work[1, ch] = split_value(turned_forward(wave, c, s))
    for ch in range(8):
        high, low = work[0, ch], work[1, ch]
        wave = dot(high, turn_ref[0]) + (dot(high, turn_ref[1]) + dot(low, turn_ref[0]))
        real, imag = joined_forward(wave)
        out_ref[ch, :OUTER] = real * (1.0 / (OUTER * INNER))
        out_ref[ch, OUTER:] = imag * (1.0 / (OUTER * INNER))


def filter_spectrum(h, first, turn, twiddle):
    return pl.pallas_call(
        filter_kernel,
        out_shape=jax.ShapeDtypeStruct((8, 2 * OUTER, INNER), F32),
        in_specs=vmem_specs(4),
        out_specs=pl.BlockSpec(memory_space=pltpu.VMEM),
        scratch_shapes=[pltpu.VMEM((2, 8, 2 * OUTER, INNER), BF16)],
        compiler_params=pltpu.CompilerParams(vmem_limit_bytes=VMEM),
        cost_estimate=pl.CostEstimate(
            flops=2 * 3 * 8 * (128 * 256 * 256 + 256 * 256 * 512), bytes_accessed=5 * MIB, transcendentals=0
        ),
    )(h, first, turn, twiddle)


def convolve_kernel(x_ref, h_ref, gain_ref, table_ref, twiddle_ref, out_ref, wide, result, work):
    c, s = twiddle_ref[0], twiddle_ref[1]
    turn, first, last = table_ref[:, :512], table_ref[:, 512:640], table_ref[:128, 640:]
    wide[...] = x_ref[...].astype(F32)
    for ch in range(8):
        row = wide[:, ch, :]
        x = jnp.concatenate([row[:, q * 256 : q * 256 + 256] for q in range(4)], 0).astype(BF16)
        work[ch] = turned_forward(dot(first, x), c, s).astype(BF16)
    for ch in range(8):
        xr, xi = joined_forward(dot(work[ch], turn))
        hr, hi = h_ref[ch, :OUTER], h_ref[ch, OUTER:]
        work[ch] = jnp.concatenate([xr * hr - xi * hi, xr * hi + xi * hr], 0).astype(BF16)
    for ch in range(8):
        r = dot(work[ch], turn)
        br = r[:OUTER, :INNER] - r[OUTER:, INNER:]
        bi = r[:OUTER, INNER:] + r[OUTER:, :INNER]
        work[ch] = jnp.concatenate([br * c - bi * s, bi * c + br * s], 0).astype(BF16)
    for ch in range(8):
        y = dot(last, work[ch])
        result[:, ch, :] = jnp.concatenate([y[q * 32 : q * 32 + 32] for q in range(4)], 1)
    out_ref[...] = (result[...] + gain_ref[...][None] * wide[...]).astype(BF16)


def convolve(x, h, gain, table, twiddle):
    return pl.pallas_call(
        convolve_kernel,
        out_shape=jax.ShapeDtypeStruct((32, 8, ROWS), BF16),
        in_specs=vmem_specs(5),
        out_specs=pl.BlockSpec(memory_space=pltpu.VMEM),
        scratch_shapes=[pltpu.VMEM((32, 8, ROWS), F32)] * 2
        + [pltpu.VMEM((8, 2 * OUTER, INNER), BF16)],
        compiler_params=pltpu.CompilerParams(vmem_limit_bytes=VMEM),
        cost_estimate=pl.CostEstimate(
            flops=2 * 8 * 2 * (128 * 256 * 256 + 256 * 256 * 512), bytes_accessed=5 * MIB, transcendentals=0
        ),
    )(x, h, gain, table, twiddle)


def finish_kernel(conv_ref, gate_ref, out_ref):
    conv = conv_ref[...].astype(F32).reshape(256, 256).T
    out_ref[...] = (conv * gate_ref[...].astype(F32)).astype(BF16)


def finish(conv, gate):
    return pl.pallas_call(
        finish_kernel,
        grid=(4,),
        out_shape=jax.ShapeDtypeStruct((ROWS, 256), BF16),
        in_specs=[
            pl.BlockSpec((32, 8, 256), lambda r: (0, 0, r)),
            pl.BlockSpec((256, 256), lambda r: (r, 0)),
        ],
        out_specs=pl.BlockSpec((256, 256), lambda r: (r, 0)),
        compiler_params=pltpu.CompilerParams(vmem_limit_bytes=8 * MIB),
        cost_estimate=pl.CostEstimate(flops=1024 * 256, bytes_accessed=2 * MIB, transcendentals=0),
    )(conv, gate)


def next_shard(x):
    return lax.ppermute(x, "ctx", [(i, i + 1) for i in range(31)])


def body(tokens, proj_weight, short_taps, long_filter, skip_gain):
    ctx, tp = lax.axis_index("ctx"), lax.axis_index("tp")
    even = ctx % 2 == 0
    first, turn, packed, twiddle = (jnp.asarray(t) for t in tables())

    q, k, v = (proj_weight[:, g] for g in range(3))
    left, right = q[:, :128], q[:, 128:]
    keep = jnp.concatenate([jnp.where(even, k, v), jnp.where(even, left, right)], 1)
    give = jnp.concatenate([jnp.where(even, v, k), jnp.where(even, right, left)], 1)
    got = lax.ppermute(give, "ctx", OTHER_CORE)
    block = jnp.concatenate([jnp.where(even, keep, got), jnp.where(even, got, keep)], 0)
    got = lax.ppermute(block, "ctx", OTHER_XHI)
    low = (ctx // 2) % 2 == 0
    block = jnp.concatenate([jnp.where(low, block, got), jnp.where(low, got, block)], 0)
    spectrum = filter_spectrum(long_filter.reshape(8, OUTER, INNER), first, turn, twiddle)

    halo = next_shard(tokens[ROWS - HALO :])
    a0 = jnp.concatenate([tokens, halo], 0)
    ap, am = from_up(a0), from_down(a0)
    b0 = other_xlo(tied(a0, block)[0])
    u1, d1 = from_above(block), from_below(block)
    w1, v1 = tied(u1, d1, ap, am)[:2]
    u2, d2 = from_above(w1), from_below(v1)
    a2 = from_up(ap)
    w2, v2 = tied(u2, d2, b0)[:2]
    bm, bp = from_down(b0), other_xlo(ap)
    u3, d3 = from_above(w2), from_below(v2)
    u4 = from_above(tied(u3, a2)[0])
    bm, bp, a2 = tied(bm, bp, a2)
    parts = (bp[:HALF], bm[HALF:])
    b2 = (from_up(parts[0]), from_down(parts[1]))
    u4, d3 = tied(u4, d3, a2, *parts)[:2]
    own = jnp.stack([block, u1, u2, u3, u4, d3, d2, d1])

    xlo, y = tp // 4, tp % 4
    mine, others = xlo * 4, (1 - xlo) * 4
    shift = lambda n: (y + n) % 4
    places = jnp.stack(
        [
            mine + y,
            mine + shift(1),
            mine + shift(3),
            others + y,
            others + shift(1),
            others + shift(3),
            mine + shift(2),
            others + shift(2),
        ]
    ).astype(jnp.int32)
    places = (places - ctx // 4) % 8
    sib = lax.ppermute(own, "ctx", OTHER_CORE)
    units = ((a0,), (ap,), (am,), (b0,), (bp,), (bm,), (a2,))
    own_acc = partial_products(places, units, own)
    taps = short_taps.transpose(1, 0, 2)
    taps_kv = jnp.where(even, taps[1:3], taps[2:0:-1])
    gated = gated_input(places, units + (b2,), own_acc, own, sib, taps_kv)

    owned = lax.all_to_all(gated, "ctx", 0, 0)
    convolved = convolve(owned, spectrum, skip_gain[:, None], packed, twiddle)
    returned = lax.all_to_all(convolved, "ctx", 0, 0)

    flag = even.astype(jnp.int32).reshape(1)
    gate = query_gate(places, flag, units + (b2,), own, sib, taps[0])
    return finish(returned, gate)


def solution(mesh):
    placed = (
        P("ctx", "tp"),
        P("ctx", None, "tp"),
        P(None, None, "tp"),
        P(("tp", "ctx"), None),
        P(("tp", "ctx")),
    )
    return jax.shard_map(
        body, mesh=mesh, in_specs=placed, out_specs=P("ctx", "tp"), check_vma=False
    )
```

```python
import functools

import jax
import jax.numpy as jnp
import numpy as np
from jax import lax
from jax.experimental import pallas as pl
from jax.experimental.pallas import tpu as pltpu
from jax.sharding import PartitionSpec as P

F32 = jnp.float32
BF16 = jnp.bfloat16
MIB = 1 << 20
VMEM = 56 * MIB

FROM_ABOVE = [(i, (i - 4) % 32) for i in range(32)]
FROM_BELOW = [(i, (i + 4) % 32) for i in range(32)]
OTHER_CORE = [(i, i ^ 1) for i in range(32)]
OTHER_XHI = [(i, i ^ 2) for i in range(32)]
OTHER_XLO = [(i, i ^ 4) for i in range(8)]
FROM_UP = [(i, (i & 4) | ((i - 1) & 3)) for i in range(8)]
FROM_DOWN = [(i, (i & 4) | ((i + 1) & 3)) for i in range(8)]
ROWS = 1024
HALF = 512
FOUR_GROUPS = [[z * 4 + r for r in range(4)] for z in range(8)]
HALO = 16
AHEAD = 8
KV = pl.ds(0, 256)
QUERY = pl.ds(256, 128)
OUTER = 128
INNER = 256


def other_xlo(x):
    return lax.ppermute(x, "tp", OTHER_XLO)


def from_up(x):
    return lax.ppermute(x, "tp", FROM_UP)


def from_down(x):
    return lax.ppermute(x, "tp", FROM_DOWN)


def from_above(x):
    return lax.ppermute(x, "ctx", FROM_ABOVE)


def from_below(x):
    return lax.ppermute(x, "ctx", FROM_BELOW)


def tied(*xs):
    return lax.optimization_barrier(xs)


def dot(a, b):
    return jnp.dot(a, b, preferred_element_type=F32)


def vmem_specs(count):
    return [pl.BlockSpec(memory_space=pltpu.VMEM)] * count


class WeightCopy:
    def __init__(self, place, pair, cols, buf, sem):
        self.place = place
        self.near = lambda: pltpu.make_async_copy(pair[0].at[jnp.minimum(place, 6), :, cols], buf, sem)
        self.far = lambda: pltpu.make_async_copy(pair[1].at[:, cols], buf, sem)

    def start(self):
        lax.cond(self.place < 7, lambda: self.near().start(), lambda: self.far().start())

    def wait(self):
        self.far().wait()


def unit_copies(places, u, units, weights, a_buf, b_buf, w_bufs, sems):
    unit = units[u]
    if len(unit) == 1:
        a, b = unit[0].at[pl.ds(0, HALF)], unit[0].at[pl.ds(HALF, HALF + HALO)]
    else:
        a, b = unit
    copies = [
        pltpu.make_async_copy(a, a_buf.at[u], sems.at[u, 0]),
        pltpu.make_async_copy(b, b_buf.at[u], sems.at[u, 1]),
    ]
    for n, ((pair, cols), buf) in enumerate(zip(weights, w_bufs)):
        copies.append(WeightCopy(places[u], pair, cols, buf.at[u], sems.at[u, 2 + n]))
    return copies


def grouped(refs, sizes):
    refs = list(refs)
    return [[refs.pop(0) for _ in range(size)] for size in sizes], refs


def flat(units):
    return [array for unit in units for array in unit]


def add_products(total, first, a, b, w):
    low = dot(a, w)
    high = dot(b, w)
    for rows, value in (
        (slice(HALO, HALO + HALF), low),
        (slice(HALO + HALF, HALO + ROWS), high[:HALF]),
        (slice(0, HALO), high[HALF:]),
    ):
        total[rows, :] = value if first else total[rows, :] + value


def sum_units(places, count, units, weights, joined, total, a_buf, b_buf, w_bufs, sems, others=()):
    copies = [
        unit_copies(places, u, units, weights, a_buf, b_buf, w_bufs, sems) for u in range(count)
    ]
    for u in range(min(AHEAD, count)):
        for copy in copies[u]:
            copy.start()
    for copy in others:
        copy.start()
    for u in range(count):
        if u + AHEAD < count:
            for copy in copies[u + AHEAD]:
                copy.start()
        for copy in copies[u]:
            copy.wait()
        add_products(total, u == 0, a_buf[u], b_buf[u], joined([buf[u] for buf in w_bufs]))


def unit_scratch(count, widths):
    return [
        pltpu.VMEM((count, HALF, 512), BF16),
        pltpu.VMEM((count, HALF + HALO, 512), BF16),
        *[pltpu.VMEM((count, 512, width), BF16) for width in widths],
        pltpu.SemaphoreType.DMA((count, 2 + len(widths))),
    ]


ANY = pl.BlockSpec(memory_space=pl.ANY)
SMEM = pl.BlockSpec(memory_space=pltpu.SMEM)


def partial_kernel(sizes, places, *refs):
    units, (near, far, out_ref, a_buf, b_buf, w_buf, sems) = grouped(refs, sizes)
    sum_units(places, 7, units, [((near, far), KV)], lambda w: w[0], out_ref, a_buf, b_buf, [w_buf], sems)


def partial_products(places, units, w):
    return pl.pallas_call(
        functools.partial(partial_kernel, [len(unit) for unit in units]),
        out_shape=jax.ShapeDtypeStruct((HALO + ROWS, 256), F32),
        in_specs=[SMEM] + [ANY] * (len(flat(units)) + 2),
        out_specs=pl.BlockSpec(memory_space=pltpu.VMEM),
        scratch_shapes=unit_scratch(7, [256]),
        compiler_params=pltpu.CompilerParams(vmem_limit_bytes=VMEM),
        cost_estimate=pl.CostEstimate(
            flops=2 * 7 * 1024 * 512 * 256, bytes_accessed=11 * MIB, transcendentals=0
        ),
    )(places, *flat(units), *w)


def filtered(branch, taps, start, size):
    total = taps[0:1, :] * branch[pl.ds(HALO + start, size), :]
    for lag in (1, 2):
        total = total + taps[lag : lag + 1, :] * branch[pl.ds(HALO + start - lag, size), :]
    return total


def rounded(branch):
    branch[...] = branch[...].astype(BF16).astype(F32)


def gated_kernel(sizes, places, *refs):
    units, refs = grouped(refs, sizes)
    acc_ref, own0, own1, sib0, sib1, taps_ref, out_ref, a_buf, b_buf, w_buf, sems = refs[:11]
    own_buf, own_sems, mine, theirs = refs[11:]
    copies = [
        pltpu.make_async_copy(acc_ref, mine, own_sems.at[0]),
        WeightCopy(places[7], (own0, own1), KV, own_buf, own_sems.at[1]),
    ]
    sum_units(places, 8, units, [((sib0, sib1), KV)], lambda w: w[0], theirs, a_buf, b_buf, [w_buf], sems, copies)
    for copy in copies:
        copy.wait()
    add_products(mine, False, a_buf[7], b_buf[7], own_buf[...])
    rounded(mine)
    rounded(theirs)
    for r in range(ROWS // 256):
        a = filtered(mine, taps_ref[0], r * 256, 256)
        b = filtered(theirs, taps_ref[1], r * 256, 256)
        out_ref[:, :, r * 256 : r * 256 + 256] = (a * b).T.reshape(32, 8, 256).astype(BF16)


def gated_input(places, units, acc, own, sib, taps):
    return pl.pallas_call(
        functools.partial(gated_kernel, [len(unit) for unit in units]),
        out_shape=jax.ShapeDtypeStruct((32, 8, ROWS), BF16),
        in_specs=[SMEM] + [ANY] * (len(flat(units)) + 5) + vmem_specs(1),
        out_specs=pl.BlockSpec(memory_space=pltpu.VMEM),
        scratch_shapes=unit_scratch(8, [256])
        + [
            pltpu.VMEM((512, 256), BF16),
            pltpu.SemaphoreType.DMA((2,)),
            pltpu.VMEM((HALO + ROWS, 256), F32),
            pltpu.VMEM((HALO + ROWS, 256), F32),
        ],
        compiler_params=pltpu.CompilerParams(vmem_limit_bytes=VMEM),
        cost_estimate=pl.CostEstimate(
            flops=2 * 9 * 1024 * 512 * 256, bytes_accessed=13 * MIB, transcendentals=0
        ),
    )(places, *flat(units), acc, *own, *sib, taps)


def query_kernel(sizes, places, even, *refs):
    units, refs = grouped(refs, sizes)
    own0, own1, sib0, sib1, taps_ref, out_ref, a_buf, b_buf, own_buf, sib_buf, sems, total = refs
    first_core = even[0] == 1

    def joined(w):
        own, sib = w
        return jnp.concatenate([jnp.where(first_core, own, sib), jnp.where(first_core, sib, own)], 1)

    sum_units(places, 8, units, [((own0, own1), QUERY), ((sib0, sib1), QUERY)], joined, total, a_buf, b_buf, [own_buf, sib_buf], sems)
    rounded(total)
    for r in range(ROWS // 256):
        out_ref[r * 256 : r * 256 + 256, :] = filtered(total, taps_ref[...], r * 256, 256).astype(BF16)


def query_gate(places, even, units, own, sib, taps):
    return pl.pallas_call(
        functools.partial(query_kernel, [len(unit) for unit in units]),
        out_shape=jax.ShapeDtypeStruct((ROWS, 256), BF16),
        in_specs=[SMEM] * 2 + [ANY] * (len(flat(units)) + 4) + vmem_specs(1),
        out_specs=pl.BlockSpec(memory_space=pltpu.VMEM),
        scratch_shapes=unit_scratch(8, [128, 128]) + [pltpu.VMEM((HALO + ROWS, 256), F32)],
        compiler_params=pltpu.CompilerParams(vmem_limit_bytes=VMEM),
        cost_estimate=pl.CostEstimate(
            flops=2 * 8 * 1024 * 512 * 256, bytes_accessed=12 * MIB, transcendentals=0
        ),
    )(places, even, *flat(units), *own, *sib, taps)


def two_parts(table):
    high = table.astype(BF16)
    return np.stack([high, (table - high.astype(np.float64)).astype(BF16)])


def tables():
    a = np.arange(OUTER, dtype=np.float64)
    b = np.arange(INNER, dtype=np.float64)
    outer = 2 * np.pi / OUTER * np.outer(a + 0.25, a)
    first = np.concatenate([np.cos(outer), -np.sin(outer)], 0)
    order = (4 * np.arange(32)[None, :] + np.arange(4)[:, None]).reshape(-1)
    inner = 2 * np.pi / INNER * (np.outer(b, b) % INNER)
    turn = np.concatenate([np.cos(inner), np.sin(inner)], 1)
    twist = 2 * np.pi / (OUTER * INNER) * np.outer(a + 0.25, b)
    twiddle = np.stack([np.cos(twist), np.sin(twist)]).astype(np.float32)
    shuffled = first[:, order].astype(BF16)
    packed = np.concatenate([turn.astype(BF16), shuffled, np.concatenate([shuffled[:, :].T, np.zeros((128, 256), BF16)], 0)], 1)
    return two_parts(first), two_parts(turn), packed, twiddle


def split_value(x):
    high = x.astype(BF16)
    return high, (x - high.astype(F32)).astype(BF16)


def turned_forward(wave, c, s):
    real, imag = wave[:OUTER], wave[OUTER:]
    return jnp.concatenate([real * c + imag * s, imag * c - real * s], 0)


def joined_forward(r):
    return r[:OUTER, :INNER] + r[OUTER:, INNER:], r[OUTER:, :INNER] - r[:OUTER, INNER:]


def filter_kernel(h_ref, first_ref, turn_ref, twiddle_ref, out_ref, work):
    c, s = twiddle_ref[0], twiddle_ref[1]
    for ch in range(8):
        high, low = split_value(h_ref[ch])
        wave = dot(first_ref[0], high) + (dot(first_ref[1], high) + dot(first_ref[0], low))
        work[0, ch], work[1, ch] = split_value(turned_forward(wave, c, s))
    for ch in range(8):
        high, low = work[0, ch], work[1, ch]
        wave = dot(high, turn_ref[0]) + (dot(high, turn_ref[1]) + dot(low, turn_ref[0]))
        real, imag = joined_forward(wave)
        out_ref[ch, :OUTER] = real * (1.0 / (OUTER * INNER))
        out_ref[ch, OUTER:] = imag * (1.0 / (OUTER * INNER))


def filter_spectrum(h, first, turn, twiddle):
    return pl.pallas_call(
        filter_kernel,
        out_shape=jax.ShapeDtypeStruct((8, 2 * OUTER, INNER), F32),
        in_specs=vmem_specs(4),
        out_specs=pl.BlockSpec(memory_space=pltpu.VMEM),
        scratch_shapes=[pltpu.VMEM((2, 8, 2 * OUTER, INNER), BF16)],
        compiler_params=pltpu.CompilerParams(vmem_limit_bytes=VMEM),
        cost_estimate=pl.CostEstimate(
            flops=2 * 3 * 8 * (128 * 256 * 256 + 256 * 256 * 512), bytes_accessed=5 * MIB, transcendentals=0
        ),
    )(h, first, turn, twiddle)


def convolve_kernel(x_ref, h_ref, gain_ref, table_ref, twiddle_ref, out_ref, wide, result, work):
    c, s = twiddle_ref[0], twiddle_ref[1]
    turn, first, last = table_ref[:, :512], table_ref[:, 512:640], table_ref[:128, 640:]
    wide[...] = x_ref[...].astype(F32)
    for ch in range(8):
        row = wide[:, ch, :]
        x = jnp.concatenate([row[:, q * 256 : q * 256 + 256] for q in range(4)], 0).astype(BF16)
        work[ch] = turned_forward(dot(first, x), c, s).astype(BF16)
    for ch in range(8):
        xr, xi = joined_forward(dot(work[ch], turn))
        hr, hi = h_ref[ch, :OUTER], h_ref[ch, OUTER:]
        work[ch] = jnp.concatenate([xr * hr - xi * hi, xr * hi + xi * hr], 0).astype(BF16)
    for ch in range(8):
        r = dot(work[ch], turn)
        br = r[:OUTER, :INNER] - r[OUTER:, INNER:]
        bi = r[:OUTER, INNER:] + r[OUTER:, :INNER]
        work[ch] = jnp.concatenate([br * c - bi * s, bi * c + br * s], 0).astype(BF16)
    for ch in range(8):
        y = dot(last, work[ch])
        result[:, ch, :] = jnp.concatenate([y[q * 32 : q * 32 + 32] for q in range(4)], 1)
    out_ref[...] = (result[...] + gain_ref[...][None] * wide[...]).astype(BF16)


def convolve(x, h, gain, table, twiddle):
    return pl.pallas_call(
        convolve_kernel,
        out_shape=jax.ShapeDtypeStruct((32, 8, ROWS), BF16),
        in_specs=vmem_specs(5),
        out_specs=pl.BlockSpec(memory_space=pltpu.VMEM),
        scratch_shapes=[pltpu.VMEM((32, 8, ROWS), F32)] * 2
        + [pltpu.VMEM((8, 2 * OUTER, INNER), BF16)],
        compiler_params=pltpu.CompilerParams(vmem_limit_bytes=VMEM),
        cost_estimate=pl.CostEstimate(
            flops=2 * 8 * 2 * (128 * 256 * 256 + 256 * 256 * 512), bytes_accessed=5 * MIB, transcendentals=0
        ),
    )(x, h, gain, table, twiddle)


def finish_kernel(conv_ref, gate_ref, out_ref):
    conv = conv_ref[...].astype(F32).reshape(256, 256).T
    out_ref[...] = (conv * gate_ref[...].astype(F32)).astype(BF16)


def finish(conv, gate):
    return pl.pallas_call(
        finish_kernel,
        grid=(4,),
        out_shape=jax.ShapeDtypeStruct((ROWS, 256), BF16),
        in_specs=[
            pl.BlockSpec((32, 8, 256), lambda r: (0, 0, r)),
            pl.BlockSpec((256, 256), lambda r: (r, 0)),
        ],
        out_specs=pl.BlockSpec((256, 256), lambda r: (r, 0)),
        compiler_params=pltpu.CompilerParams(vmem_limit_bytes=8 * MIB),
        cost_estimate=pl.CostEstimate(flops=1024 * 256, bytes_accessed=2 * MIB, transcendentals=0),
    )(conv, gate)


def next_shard(x):
    return lax.ppermute(x, "ctx", [(i, i + 1) for i in range(31)])


def body(tokens, proj_weight, short_taps, long_filter, skip_gain):
    ctx, tp = lax.axis_index("ctx"), lax.axis_index("tp")
    even = ctx % 2 == 0
    first, turn, packed, twiddle = (jnp.asarray(t) for t in tables())

    q, k, v = (proj_weight[:, g] for g in range(3))
    left, right = q[:, :128], q[:, 128:]
    keep = jnp.concatenate([jnp.where(even, k, v), jnp.where(even, left, right)], 1)
    give = jnp.concatenate([jnp.where(even, v, k), jnp.where(even, right, left)], 1)
    got = lax.ppermute(give, "ctx", OTHER_CORE)
    block = jnp.concatenate([jnp.where(even, keep, got), jnp.where(even, got, keep)], 0)
    got = lax.ppermute(block, "ctx", OTHER_XHI)
    low = (ctx // 2) % 2 == 0
    block = jnp.concatenate([jnp.where(low, block, got), jnp.where(low, got, block)], 0)
    spectrum = filter_spectrum(long_filter.reshape(8, OUTER, INNER), first, turn, twiddle)

    halo = next_shard(tokens[ROWS - HALO :])
    a0 = jnp.concatenate([tokens, halo], 0)
    ap, am = from_up(a0), from_down(a0)
    b0 = other_xlo(tied(a0, block)[0])
    u1, d1 = from_above(block), from_below(block)
    w1, v1 = tied(u1, d1, ap, am)[:2]
    u2, d2 = from_above(w1), from_below(v1)
    a2 = from_up(ap)
    w2, v2 = tied(u2, d2, b0)[:2]
    bm, bp = from_down(b0), other_xlo(ap)
    u3, d3 = from_above(w2), from_below(v2)
    a2, bm, bp, u3, d3 = tied(a2, bm, bp, u3, d3)
    b2 = (from_up(bp[:HALF]), from_down(bm[HALF:]))
    far = jnp.concatenate([from_above(u3[:256]), from_below(d3[256:])], 0)
    own = (jnp.stack([block, u1, u2, u3, d3, d2, d1]), far)

    xlo, y = tp // 4, tp % 4
    mine, others = xlo * 4, (1 - xlo) * 4
    shift = lambda n: (y + n) % 4
    places = jnp.stack(
        [
            mine + y,
            mine + shift(1),
            mine + shift(3),
            others + y,
            others + shift(1),
            others + shift(3),
            mine + shift(2),
            others + shift(2),
        ]
    ).astype(jnp.int32)
    places = (places - ctx // 4) % 8
    places = jnp.where(places == 4, 7, jnp.where(places > 4, places - 1, places))
    sib = tuple(lax.ppermute(w, "ctx", OTHER_CORE) for w in own)
    units = ((a0,), (ap,), (am,), (b0,), (bp,), (bm,), (a2,))
    own_acc = partial_products(places, units, own)
    taps = short_taps.transpose(1, 0, 2)
    taps_kv = jnp.where(even, taps[1:3], taps[2:0:-1])
    gated = gated_input(places, units + (b2,), own_acc, own, sib, taps_kv)

    owned = lax.all_to_all(gated, "ctx", 0, 0)
    convolved = convolve(owned, spectrum, skip_gain[:, None], packed, twiddle)
    returned = lax.all_to_all(convolved, "ctx", 0, 0)

    flag = even.astype(jnp.int32).reshape(1)
    gate = query_gate(places, flag, units + (b2,), own, sib, taps[0])
    return finish(returned, gate)


def solution(mesh):
    placed = (
        P("ctx", "tp"),
        P("ctx", None, "tp"),
        P(None, None, "tp"),
        P(("tp", "ctx"), None),
        P(("tp", "ctx")),
    )
    return jax.shard_map(
        body, mesh=mesh, in_specs=placed, out_specs=P("ctx", "tp"), check_vma=False
    )
```

```python
import functools

import jax
import jax.numpy as jnp
import numpy as np
from jax import lax
from jax.experimental import pallas as pl
from jax.experimental.pallas import tpu as pltpu
from jax.sharding import PartitionSpec as P

F32 = jnp.float32
BF16 = jnp.bfloat16
MIB = 1 << 20
VMEM = 56 * MIB

FROM_ABOVE = [(i, (i - 4) % 32) for i in range(32)]
FROM_BELOW = [(i, (i + 4) % 32) for i in range(32)]
OTHER_CORE = [(i, i ^ 1) for i in range(32)]
OTHER_XHI = [(i, i ^ 2) for i in range(32)]
OTHER_XLO = [(i, i ^ 4) for i in range(8)]
FROM_UP = [(i, (i & 4) | ((i - 1) & 3)) for i in range(8)]
FROM_DOWN = [(i, (i & 4) | ((i + 1) & 3)) for i in range(8)]
ROWS = 1024
HALF = 512
FOUR_GROUPS = [[z * 4 + r for r in range(4)] for z in range(8)]
HALO = 16
AHEAD = 8
KV = pl.ds(0, 256)
QUERY = pl.ds(256, 128)
OUTER = 128
INNER = 256


def other_xlo(x):
    return lax.ppermute(x, "tp", OTHER_XLO)


def from_up(x):
    return lax.ppermute(x, "tp", FROM_UP)


def from_down(x):
    return lax.ppermute(x, "tp", FROM_DOWN)


def from_above(x):
    return lax.ppermute(x, "ctx", FROM_ABOVE)


def from_below(x):
    return lax.ppermute(x, "ctx", FROM_BELOW)


def tied(*xs):
    return lax.optimization_barrier(xs)


def dot(a, b):
    return jnp.dot(a, b, preferred_element_type=F32)


def vmem_specs(count):
    return [pl.BlockSpec(memory_space=pltpu.VMEM)] * count


class WeightCopy:
    def __init__(self, place, pair, cols, buf, sem):
        self.place = place
        self.near = lambda: pltpu.make_async_copy(pair[0].at[jnp.minimum(place, 6), :, cols], buf, sem)
        self.far = lambda: pltpu.make_async_copy(pair[1].at[:, cols], buf, sem)

    def start(self):
        lax.cond(self.place < 7, lambda: self.near().start(), lambda: self.far().start())

    def wait(self):
        self.far().wait()


def unit_copies(places, u, units, weights, a_buf, b_buf, w_bufs, sems):
    unit = units[u]
    if len(unit) == 1:
        a, b = unit[0].at[pl.ds(0, HALF)], unit[0].at[pl.ds(HALF, HALF + HALO)]
    else:
        a, b = unit
    copies = [
        pltpu.make_async_copy(a, a_buf.at[u], sems.at[u, 0]),
        pltpu.make_async_copy(b, b_buf.at[u], sems.at[u, 1]),
    ]
    for n, ((pair, cols), buf) in enumerate(zip(weights, w_bufs)):
        copies.append(WeightCopy(places[u], pair, cols, buf.at[u], sems.at[u, 2 + n]))
    return copies


def grouped(refs, sizes):
    refs = list(refs)
    return [[refs.pop(0) for _ in range(size)] for size in sizes], refs


def flat(units):
    return [array for unit in units for array in unit]


def add_products(total, first, a, b, w):
    low = dot(a, w)
    high = dot(b, w)
    for rows, value in (
        (slice(HALO, HALO + HALF), low),
        (slice(HALO + HALF, HALO + ROWS), high[:HALF]),
        (slice(0, HALO), high[HALF:]),
    ):
        total[rows, :] = value if first else total[rows, :] + value


def sum_units(places, count, units, weights, joined, total, a_buf, b_buf, w_bufs, sems, others=()):
    copies = [
        unit_copies(places, u, units, weights, a_buf, b_buf, w_bufs, sems) for u in range(count)
    ]
    for u in range(min(AHEAD, count)):
        for copy in copies[u]:
            copy.start()
    for copy in others:
        copy.start()
    for u in range(count):
        if u + AHEAD < count:
            for copy in copies[u + AHEAD]:
                copy.start()
        for copy in copies[u]:
            copy.wait()
        add_products(total, u == 0, a_buf[u], b_buf[u], joined([buf[u] for buf in w_bufs]))


def unit_scratch(count, widths):
    return [
        pltpu.VMEM((count, HALF, 512), BF16),
        pltpu.VMEM((count, HALF + HALO, 512), BF16),
        *[pltpu.VMEM((count, 512, width), BF16) for width in widths],
        pltpu.SemaphoreType.DMA((count, 2 + len(widths))),
    ]


ANY = pl.BlockSpec(memory_space=pl.ANY)
SMEM = pl.BlockSpec(memory_space=pltpu.SMEM)


def partial_kernel(sizes, places, *refs):
    units, refs = grouped(refs, sizes)
    own0, own1, sib0, sib1, out_ref, a_buf, b_buf, own_buf, sib_buf, sems = refs
    weights = [((own0, own1), KV), ((sib0, sib1), KV)]
    joined = lambda w: jnp.concatenate(w, 1)
    sum_units(places, 7, units, weights, joined, out_ref, a_buf, b_buf, [own_buf, sib_buf], sems)


def partial_products(places, units, own, sib):
    return pl.pallas_call(
        functools.partial(partial_kernel, [len(unit) for unit in units]),
        out_shape=jax.ShapeDtypeStruct((HALO + ROWS, 512), F32),
        in_specs=[SMEM] + [ANY] * (len(flat(units)) + 4),
        out_specs=pl.BlockSpec(memory_space=pltpu.VMEM),
        scratch_shapes=unit_scratch(7, [256, 256]),
        compiler_params=pltpu.CompilerParams(vmem_limit_bytes=VMEM),
        cost_estimate=pl.CostEstimate(
            flops=2 * 7 * 1024 * 512 * 512, bytes_accessed=13 * MIB, transcendentals=0
        ),
    )(places, *flat(units), *own, *sib)


def filtered(branch, taps, start, size):
    total = taps[0:1, :] * branch[pl.ds(HALO + start, size), :]
    for lag in (1, 2):
        total = total + taps[lag : lag + 1, :] * branch[pl.ds(HALO + start - lag, size), :]
    return total


def rounded(branch):
    branch[...] = branch[...].astype(BF16).astype(F32)


def gated_kernel(places, a_ref, b_ref, acc_ref, own0, own1, sib0, sib1, taps_ref, out_ref, *scratch):
    a_buf, b_buf, own_buf, sib_buf, total, sems = scratch
    copies = [
        WeightCopy(places[7], (own0, own1), KV, own_buf, sems.at[0]),
        WeightCopy(places[7], (sib0, sib1), KV, sib_buf, sems.at[1]),
        pltpu.make_async_copy(a_ref, a_buf, sems.at[2]),
        pltpu.make_async_copy(b_ref, b_buf, sems.at[3]),
        pltpu.make_async_copy(acc_ref, total, sems.at[4]),
    ]
    for copy in copies:
        copy.start()
    for copy in copies:
        copy.wait()
    w = jnp.concatenate([own_buf[...], sib_buf[...]], 1)
    add_products(total, False, a_buf[...], b_buf[...], w)
    rounded(total)
    taps = jnp.concatenate([taps_ref[0], taps_ref[1]], 1)
    for r in range(ROWS // 256):
        mixed = filtered(total, taps, r * 256, 256)
        product = mixed[:, :256] * mixed[:, 256:]
        out_ref[:, :, r * 256 : r * 256 + 256] = product.T.reshape(32, 8, 256).astype(BF16)


def gated_input(places, last, acc, own, sib, taps):
    return pl.pallas_call(
        gated_kernel,
        out_shape=jax.ShapeDtypeStruct((32, 8, ROWS), BF16),
        in_specs=[SMEM] + [ANY] * 7 + vmem_specs(1),
        out_specs=pl.BlockSpec(memory_space=pltpu.VMEM),
        scratch_shapes=[
            pltpu.VMEM((HALF, 512), BF16),
            pltpu.VMEM((HALF + HALO, 512), BF16),
            pltpu.VMEM((512, 256), BF16),
            pltpu.VMEM((512, 256), BF16),
            pltpu.VMEM((HALO + ROWS, 512), F32),
            pltpu.SemaphoreType.DMA((5,)),
        ],
        compiler_params=pltpu.CompilerParams(vmem_limit_bytes=VMEM),
        cost_estimate=pl.CostEstimate(
            flops=2 * 1024 * 512 * 512, bytes_accessed=5 * MIB, transcendentals=0
        ),
    )(places, *last, acc, *own, *sib, taps)


def query_kernel(sizes, places, even, *refs):
    units, refs = grouped(refs, sizes)
    own0, own1, sib0, sib1, taps_ref, out_ref, a_buf, b_buf, own_buf, sib_buf, sems, total = refs
    first_core = even[0] == 1

    def joined(w):
        own, sib = w
        return jnp.concatenate([jnp.where(first_core, own, sib), jnp.where(first_core, sib, own)], 1)

    sum_units(places, 8, units, [((own0, own1), QUERY), ((sib0, sib1), QUERY)], joined, total, a_buf, b_buf, [own_buf, sib_buf], sems)
    rounded(total)
    for r in range(ROWS // 256):
        out_ref[r * 256 : r * 256 + 256, :] = filtered(total, taps_ref[...], r * 256, 256).astype(BF16)


def query_gate(places, even, units, own, sib, taps):
    return pl.pallas_call(
        functools.partial(query_kernel, [len(unit) for unit in units]),
        out_shape=jax.ShapeDtypeStruct((ROWS, 256), BF16),
        in_specs=[SMEM] * 2 + [ANY] * (len(flat(units)) + 4) + vmem_specs(1),
        out_specs=pl.BlockSpec(memory_space=pltpu.VMEM),
        scratch_shapes=unit_scratch(8, [128, 128]) + [pltpu.VMEM((HALO + ROWS, 256), F32)],
        compiler_params=pltpu.CompilerParams(vmem_limit_bytes=VMEM),
        cost_estimate=pl.CostEstimate(
            flops=2 * 8 * 1024 * 512 * 256, bytes_accessed=12 * MIB, transcendentals=0
        ),
    )(places, even, *flat(units), *own, *sib, taps)


def two_parts(table):
    high = table.astype(BF16)
    return np.stack([high, (table - high.astype(np.float64)).astype(BF16)])


def tables():
    a = np.arange(OUTER, dtype=np.float64)
    b = np.arange(INNER, dtype=np.float64)
    outer = 2 * np.pi / OUTER * np.outer(a + 0.25, a)
    first = np.concatenate([np.cos(outer), -np.sin(outer)], 0)
    order = (4 * np.arange(32)[None, :] + np.arange(4)[:, None]).reshape(-1)
    inner = 2 * np.pi / INNER * (np.outer(b, b) % INNER)
    turn = np.concatenate([np.cos(inner), np.sin(inner)], 1)
    twist = 2 * np.pi / (OUTER * INNER) * np.outer(a + 0.25, b)
    twiddle = np.stack([np.cos(twist), np.sin(twist)]).astype(np.float32)
    shuffled = first[:, order].astype(BF16)
    packed = np.concatenate([turn.astype(BF16), shuffled, np.concatenate([shuffled[:, :].T, np.zeros((128, 256), BF16)], 0)], 1)
    return two_parts(first), two_parts(turn), packed, twiddle


def split_value(x):
    high = x.astype(BF16)
    return high, (x - high.astype(F32)).astype(BF16)


def turned_forward(wave, c, s):
    real, imag = wave[:OUTER], wave[OUTER:]
    return jnp.concatenate([real * c + imag * s, imag * c - real * s], 0)


def joined_forward(r):
    return r[:OUTER, :INNER] + r[OUTER:, INNER:], r[OUTER:, :INNER] - r[:OUTER, INNER:]


def filter_kernel(h_ref, first_ref, turn_ref, twiddle_ref, out_ref, work):
    c, s = twiddle_ref[0], twiddle_ref[1]
    for ch in range(8):
        high, low = split_value(h_ref[ch])
        wave = dot(first_ref[0], high) + (dot(first_ref[1], high) + dot(first_ref[0], low))
        work[0, ch], work[1, ch] = split_value(turned_forward(wave, c, s))
    for ch in range(8):
        high, low = work[0, ch], work[1, ch]
        wave = dot(high, turn_ref[0]) + (dot(high, turn_ref[1]) + dot(low, turn_ref[0]))
        real, imag = joined_forward(wave)
        out_ref[ch, :OUTER] = real * (1.0 / (OUTER * INNER))
        out_ref[ch, OUTER:] = imag * (1.0 / (OUTER * INNER))


def filter_spectrum(h, first, turn, twiddle):
    return pl.pallas_call(
        filter_kernel,
        out_shape=jax.ShapeDtypeStruct((8, 2 * OUTER, INNER), F32),
        in_specs=vmem_specs(4),
        out_specs=pl.BlockSpec(memory_space=pltpu.VMEM),
        scratch_shapes=[pltpu.VMEM((2, 8, 2 * OUTER, INNER), BF16)],
        compiler_params=pltpu.CompilerParams(vmem_limit_bytes=VMEM),
        cost_estimate=pl.CostEstimate(
            flops=2 * 3 * 8 * (128 * 256 * 256 + 256 * 256 * 512), bytes_accessed=5 * MIB, transcendentals=0
        ),
    )(h, first, turn, twiddle)


def convolve_kernel(x_ref, h_ref, gain_ref, table_ref, twiddle_ref, out_ref, wide, result, work):
    c, s = twiddle_ref[0], twiddle_ref[1]
    turn, first, last = table_ref[:, :512], table_ref[:, 512:640], table_ref[:128, 640:]
    wide[...] = x_ref[...].astype(F32)
    for ch in range(8):
        row = wide[:, ch, :]
        x = jnp.concatenate([row[:, q * 256 : q * 256 + 256] for q in range(4)], 0).astype(BF16)
        work[ch] = turned_forward(dot(first, x), c, s).astype(BF16)
    for ch in range(8):
        xr, xi = joined_forward(dot(work[ch], turn))
        hr, hi = h_ref[ch, :OUTER], h_ref[ch, OUTER:]
        work[ch] = jnp.concatenate([xr * hr - xi * hi, xr * hi + xi * hr], 0).astype(BF16)
    for ch in range(8):
        r = dot(work[ch], turn)
        br = r[:OUTER, :INNER] - r[OUTER:, INNER:]
        bi = r[:OUTER, INNER:] + r[OUTER:, :INNER]
        work[ch] = jnp.concatenate([br * c - bi * s, bi * c + br * s], 0).astype(BF16)
    for ch in range(8):
        y = dot(last, work[ch])
        result[:, ch, :] = jnp.concatenate([y[q * 32 : q * 32 + 32] for q in range(4)], 1)
    out_ref[...] = (result[...] + gain_ref[...][None] * wide[...]).astype(BF16)


def convolve(x, h, gain, table, twiddle):
    return pl.pallas_call(
        convolve_kernel,
        out_shape=jax.ShapeDtypeStruct((32, 8, ROWS), BF16),
        in_specs=vmem_specs(5),
        out_specs=pl.BlockSpec(memory_space=pltpu.VMEM),
        scratch_shapes=[pltpu.VMEM((32, 8, ROWS), F32)] * 2
        + [pltpu.VMEM((8, 2 * OUTER, INNER), BF16)],
        compiler_params=pltpu.CompilerParams(vmem_limit_bytes=VMEM),
        cost_estimate=pl.CostEstimate(
            flops=2 * 8 * 2 * (128 * 256 * 256 + 256 * 256 * 512), bytes_accessed=5 * MIB, transcendentals=0
        ),
    )(x, h, gain, table, twiddle)


def finish_kernel(conv_ref, gate_ref, out_ref):
    conv = conv_ref[...].astype(F32).reshape(256, 256).T
    out_ref[...] = (conv * gate_ref[...].astype(F32)).astype(BF16)


def finish(conv, gate):
    return pl.pallas_call(
        finish_kernel,
        grid=(4,),
        out_shape=jax.ShapeDtypeStruct((ROWS, 256), BF16),
        in_specs=[
            pl.BlockSpec((32, 8, 256), lambda r: (0, 0, r)),
            pl.BlockSpec((256, 256), lambda r: (r, 0)),
        ],
        out_specs=pl.BlockSpec((256, 256), lambda r: (r, 0)),
        compiler_params=pltpu.CompilerParams(vmem_limit_bytes=8 * MIB),
        cost_estimate=pl.CostEstimate(flops=1024 * 256, bytes_accessed=2 * MIB, transcendentals=0),
    )(conv, gate)


def next_shard(x):
    return lax.ppermute(x, "ctx", [(i, i + 1) for i in range(31)])


def body(tokens, proj_weight, short_taps, long_filter, skip_gain):
    ctx, tp = lax.axis_index("ctx"), lax.axis_index("tp")
    even = ctx % 2 == 0
    first, turn, packed, twiddle = (jnp.asarray(t) for t in tables())

    q, k, v = (proj_weight[:, g] for g in range(3))
    left, right = q[:, :128], q[:, 128:]
    keep = jnp.concatenate([jnp.where(even, k, v), jnp.where(even, left, right)], 1)
    give = jnp.concatenate([jnp.where(even, v, k), jnp.where(even, right, left)], 1)
    got = lax.ppermute(give, "ctx", OTHER_CORE)
    block = jnp.concatenate([jnp.where(even, keep, got), jnp.where(even, got, keep)], 0)
    got = lax.ppermute(block, "ctx", OTHER_XHI)
    low = (ctx // 2) % 2 == 0
    block = jnp.concatenate([jnp.where(low, block, got), jnp.where(low, got, block)], 0)
    spectrum = filter_spectrum(long_filter.reshape(8, OUTER, INNER), first, turn, twiddle)

    halo = next_shard(tokens[ROWS - HALO :])
    a0 = jnp.concatenate([tokens, halo], 0)
    ap, am = from_up(a0), from_down(a0)
    b0 = other_xlo(tied(a0, block)[0])
    u1, d1 = from_above(block), from_below(block)
    w1, v1 = tied(u1, d1, ap, am)[:2]
    u2, d2 = from_above(w1), from_below(v1)
    a2 = from_up(ap)
    w2, v2 = tied(u2, d2, b0)[:2]
    bm, bp = from_down(b0), other_xlo(ap)
    u3, d3 = from_above(w2), from_below(v2)
    a2, bm, bp, u3, d3 = tied(a2, bm, bp, u3, d3)
    b2 = (from_up(bp[:HALF]), from_down(bm[HALF:]))
    far = jnp.concatenate([from_above(u3[:256]), from_below(d3[256:])], 0)
    own = (jnp.stack([block, u1, u2, u3, d3, d2, d1]), far)

    xlo, y = tp // 4, tp % 4
    mine, others = xlo * 4, (1 - xlo) * 4
    shift = lambda n: (y + n) % 4
    places = jnp.stack(
        [
            mine + y,
            mine + shift(1),
            mine + shift(3),
            others + y,
            others + shift(1),
            others + shift(3),
            mine + shift(2),
            others + shift(2),
        ]
    ).astype(jnp.int32)
    places = (places - ctx // 4) % 8
    places = jnp.where(places == 4, 7, jnp.where(places > 4, places - 1, places))
    sib = tuple(lax.ppermute(w, "ctx", OTHER_CORE) for w in own)
    units = ((a0,), (ap,), (am,), (b0,), (bp,), (bm,), (a2,))
    acc = partial_products(places, units, own, sib)
    taps = short_taps.transpose(1, 0, 2)
    taps_kv = jnp.where(even, taps[1:3], taps[2:0:-1])
    gated = gated_input(places, b2, acc, own, sib, taps_kv)

    owned = lax.all_to_all(gated, "ctx", 0, 0)
    convolved = convolve(owned, spectrum, skip_gain[:, None], packed, twiddle)
    returned = lax.all_to_all(convolved, "ctx", 0, 0)

    flag = even.astype(jnp.int32).reshape(1)
    gate = query_gate(places, flag, units + (b2,), own, sib, taps[0])
    return finish(returned, gate)


def solution(mesh):
    placed = (
        P("ctx", "tp"),
        P("ctx", None, "tp"),
        P(None, None, "tp"),
        P(("tp", "ctx"), None),
        P(("tp", "ctx")),
    )
    return jax.shard_map(
        body, mesh=mesh, in_specs=placed, out_specs=P("ctx", "tp"), check_vma=False
    )
```
